32 devices in a mesh: grp: 2 (over y), freq: 4 (over z), tm: 2 (over x), pol: 2 (over core).
Axes of the slice: x: 2, y: 2, z: 4, core: 2. Of those that a mesh axis runs over, the one named last changes fastest.
Arguments:
- voltages: bfloat16 [2, 8, 1024, 4, 2, 256], P('pol', ('grp', 'freq'), 'tm'), parts along dimension 1, may hold values from -6 to 6
- feed_gains: float32 [8, 2, 4, 2, 256], P(('grp', 'freq'), 'pol'), parts along dimension 0, may hold values from -5 to 5
- owner_table: int32 [64], replicated, may hold values from 0 to 3, as said below
- keep_flags: int32 [1024], replicated, may hold values 0 or 1
Outputs:
- owned: bfloat16 [128, 64, 2048], P(('grp', 'tm', 'pol'), None, 'freq'), parts along dimension 0
The draws below stay inside these ranges and needn't reach their ends.
There are 2 independent parts, one for each index of `grp`. The reference program is written for one: setup_inputs(seed, part) draws one part's arguments, and reference() takes and returns one part's arrays. A program takes and returns all parts, laid end to end along the dimension named above; an argument that names none is the same for every part. Nothing has to cross between parts.
Inputs may be any that keep to these rules, and one draw needn't show every extreme that they name: `owner_table`: each index of freq owns from 0 to 32 beam sets; one owns exactly 32.
All inputs are finite; a program needn't handle non-finite values.
Results may differ from the reference program's by a relative error of at most 0.0058.
Values may be sent and summed in bfloat16 or wider, within the bound.
A program may use at most 64 MiB of HBM per device.

```python
import jax
import jax.numpy as jnp
from jax import lax

NS = 256
CYL = 4
UPCH = 16
TAPS = 16
SET_BEAMS = 16
BEAMS = 1024
SETS = 64
MOST = 32
CHANNELS = 4
FRAMES = 64
SAMPLES = 1024
N_FREQ = 4


def draw_owner_table(key, part):
    key_big = jax.random.fold_in(key, 11)
    key_slots = jax.random.fold_in(key, 23)
    key_order = jax.random.fold_in(key, 37)
    biggest = jax.random.randint(key_big, (), 0, N_FREQ).astype(jnp.int32)
    others = (biggest + 1 + jnp.arange(N_FREQ - 1, dtype=jnp.int32)) % N_FREQ
    shuffled = jax.random.permutation(key_slots, (N_FREQ - 1) * MOST)
    chosen = shuffled[:SETS - MOST]
    extra_owner = jnp.take(others, chosen // MOST)
    sequence = jnp.concatenate([jnp.zeros((MOST,), jnp.int32) + biggest, extra_owner.astype(jnp.int32)])
    order = jax.random.permutation(key_order, SETS)
    return jnp.take(sequence, order).astype(jnp.int32)


def plant(entries, stream_key, smallest, largest):
    shape = entries.shape
    spot = [jax.random.randint(jax.random.fold_in(stream_key, axis), (), 0, shape[axis]) for axis in range(len(shape))]
    entries = entries.at[tuple(spot)].set(smallest)
    longest = shape.index(max(shape))
    spot[longest] = (spot[longest] + 1) % shape[longest]
    return entries.at[tuple(spot)].set(largest)


def shard_levels(own_key, extent, cuts, low, high):
    level = 1.0
    for axis_at, parts in cuts:
        draws = jax.random.uniform(jax.random.fold_in(jax.random.fold_in(own_key, 6), axis_at), (parts,), jnp.float32, low / len(cuts), high / len(cuts))
        level = level * jnp.repeat(jnp.exp(draws), extent[axis_at] // parts).reshape((-1,) + (1,) * (len(extent) - 1 - axis_at))
    return level


def centred(own_key, extent, spread, limit, cuts=(), kind=jnp.bfloat16):
    result = jax.random.normal(own_key, extent, jnp.float32) * spread
    if len(cuts) > 0:
        result = shard_levels(own_key, extent, cuts, -0.22, 0.18) * result
    return jnp.clip(result, min=-limit, max=limit).astype(kind)


def setup_inputs(seed: int = 0, part: int = 0) -> dict:
    key_list = jax.random.split(jax.random.key(seed), 5)
    own_keys = jax.random.split(jax.random.fold_in(key_list[4], part), 5)
    voltages = centred(own_keys[0], (2, CHANNELS, SAMPLES, CYL, 2, NS), 1.0, 6.0, ((0, 2), (1, 4), (2, 2)))
    feed_gains = centred(own_keys[1], (CHANNELS, 2, CYL, 2, NS), 1.0, 5.0, ((0, 4), (1, 2)), jnp.float32)
    owner_table = draw_owner_table(jax.random.fold_in(key_list[4], 71), part)
    keep_flags = plant((jax.random.randint(key_list[3], (BEAMS,), 0, 4) < 3).astype(jnp.int32), jax.random.fold_in(key_list[3], 1), 0, 1)
    return dict(voltages=voltages, feed_gains=feed_gains, owner_table=owner_table, keep_flags=keep_flags)


def window_taps():
    span = TAPS * UPCH
    steps = jnp.arange(span, dtype=jnp.float32)
    weights = jnp.sinc((steps - (span - 1) / 2.0) / UPCH) * jnp.sin(jnp.pi * (steps + 0.5) / span) ** 2
    weights = weights / jnp.sqrt(jnp.sum(weights * weights))
    return weights.reshape(TAPS, UPCH)

def fine_tables():
    rows = jnp.arange(UPCH, dtype=jnp.int32)
    phase = rows[:, None] * rows[None, :] % UPCH
    angle = 2.0 * jnp.pi * phase.astype(jnp.float32) / UPCH
    return (jnp.cos(angle), jnp.sin(angle))

def beam_matrix():
    rows = jnp.arange(NS, dtype=jnp.int32)
    phase = rows[:, None] * rows[None, :] % NS
    angle = 2.0 * jnp.pi * phase.astype(jnp.float32) / NS
    scale = 1.0 / jnp.sqrt(jnp.float32(NS))
    cosine = jnp.cos(angle) * scale
    sine = jnp.sin(angle) * scale
    upper = jnp.concatenate([cosine, -sine], axis=1)
    lower = jnp.concatenate([sine, cosine], axis=1)
    return jnp.concatenate([upper, lower], axis=0).astype(jnp.bfloat16)

def cylinder_tables():
    rows = jnp.arange(CYL, dtype=jnp.int32)
    phase = rows[:, None] * rows[None, :] % CYL
    angle = 2.0 * jnp.pi * phase.astype(jnp.float32) / CYL
    return (0.5 * jnp.cos(angle), 0.5 * jnp.sin(angle))

def power_frames(frames, gain_pol, n_out):
    window = window_taps()
    fine_cos, fine_sin = fine_tables()
    beam_table = beam_matrix()
    cyl_cos, cyl_sin = cylinder_tables()
    highest = lax.Precision.HIGHEST
    chan_count = frames.shape[0]
    summed = jnp.zeros((chan_count, n_out) + frames.shape[2:], jnp.float32)
    for tap_index in range(TAPS):
        weights = window[tap_index].reshape(1, 1, UPCH, 1, 1, 1)
        summed = summed + weights * frames[:, tap_index:tap_index + n_out].astype(jnp.float32)
    real_part = summed[:, :, :, :, 0, :]
    imag_part = summed[:, :, :, :, 1, :]
    spec_real = jnp.einsum('qk,cmkxn->mcqxn', fine_cos, real_part, precision=highest) + jnp.einsum('qk,cmkxn->mcqxn', fine_sin, imag_part, precision=highest)
    spec_imag = jnp.einsum('qk,cmkxn->mcqxn', fine_cos, imag_part, precision=highest) - jnp.einsum('qk,cmkxn->mcqxn', fine_sin, real_part, precision=highest)
    gain_real = gain_pol[:, :, 0, :][None, :, None]
    gain_imag = gain_pol[:, :, 1, :][None, :, None]
    cal_real = spec_real * gain_real - spec_imag * gain_imag
    cal_imag = spec_real * gain_imag + spec_imag * gain_real
    calibrated = jnp.stack([cal_real, cal_imag], axis=4).astype(jnp.bfloat16)
    row_count = n_out * chan_count * UPCH
    flat = calibrated.reshape(row_count * CYL, 2 * NS)
    partial_value = jnp.dot(flat.astype(jnp.float32), beam_table.astype(jnp.float32), precision=highest, preferred_element_type=jnp.float32)
    partial_value = partial_value.reshape(row_count, CYL, 2, NS)
    beam_real = partial_value[:, :, 0, :]
    beam_imag = partial_value[:, :, 1, :]
    form_real = jnp.einsum('ec,rcn->ren', cyl_cos, beam_real, precision=highest) + jnp.einsum('ec,rcn->ren', cyl_sin, beam_imag, precision=highest)
    form_imag = jnp.einsum('ec,rcn->ren', cyl_cos, beam_imag, precision=highest) - jnp.einsum('ec,rcn->ren', cyl_sin, beam_real, precision=highest)
    powers = (form_real * form_real + form_imag * form_imag).astype(jnp.bfloat16)
    return powers.reshape(n_out, chan_count * UPCH, CYL * NS)

def slot_columns(owner_table, keep_flags, n_owner, most_sets):
    count = owner_table.shape[0]
    order = jnp.arange(count, dtype=jnp.int32)
    same_owner = owner_table[:, None] == owner_table[None, :]
    earlier = order[None, :] < order[:, None]
    set_rank = lax.optimization_barrier(jnp.sum(jnp.logical_and(same_owner, earlier).astype(jnp.int32), axis=1))
    slot_index = owner_table * most_sets + set_rank
    places = jnp.arange(n_owner * most_sets, dtype=jnp.int32)
    matches = (slot_index[None, :] == places[:, None]).astype(jnp.int32)
    filled = lax.optimization_barrier(jnp.sum(matches, axis=1))
    set_of = lax.optimization_barrier(jnp.sum(matches * order[None, :], axis=1))
    within = jnp.arange(SET_BEAMS, dtype=jnp.int32)
    beam_index = (set_of[:, None] * SET_BEAMS + within[None, :]).reshape(-1).astype(jnp.int32)
    kept = jnp.take(keep_flags, beam_index).reshape(-1, SET_BEAMS)
    column_mask = (filled[:, None] * kept).reshape(-1)
    return (beam_index, column_mask)

def reference(voltages, feed_gains, owner_table, keep_flags):
    pad_count = (TAPS - 1) * UPCH

    def one_channel(chan_index):
        volts_here = lax.dynamic_index_in_dim(voltages, chan_index, 1, keepdims=False)
        gains_here = lax.dynamic_index_in_dim(feed_gains, chan_index, 0, keepdims=False)
        summed = jnp.zeros((FRAMES, UPCH, CYL * NS), jnp.float32)
        for pol_index in range(2):
            padded = jnp.concatenate([jnp.zeros((pad_count, CYL, 2, NS), jnp.bfloat16), volts_here[pol_index]], axis=0)
            frames = padded.reshape(1, FRAMES + TAPS - 1, UPCH, CYL, 2, NS)
            summed = summed + power_frames(frames, gains_here[pol_index][None], FRAMES).astype(jnp.float32)
        return summed.astype(jnp.bfloat16)
    per_channel = lax.map(one_channel, jnp.arange(CHANNELS, dtype=jnp.int32))
    intensity = jnp.transpose(per_channel, (1, 0, 2, 3)).reshape(FRAMES, CHANNELS * UPCH, CYL * NS)
    beam_index, column_mask = slot_columns(owner_table, keep_flags, N_FREQ, MOST)
    return jnp.take(intensity, beam_index, axis=2) * column_mask.astype(jnp.bfloat16)[None, None, :]
```

```python
import functools

import jax
import jax.numpy as jnp
import ml_dtypes
import numpy as np
from jax import lax
from jax.experimental import pallas as pl
from jax.experimental.pallas import tpu as pltpu
from jax.sharding import PartitionSpec as P

NS = 256
CYL = 4
UPCH = 16
TAPS = 16
SET_BEAMS = 16
GROUP = 8
ROWS = GROUP * UPCH
WIDE = GROUP * UPCH * 2
BEAMS = CYL * NS


def window_taps():
    span = TAPS * UPCH
    steps = np.arange(span, dtype=np.float64)
    weights = np.sinc((steps - (span - 1) / 2.0) / UPCH) * np.sin(np.pi * (steps + 0.5) / span) ** 2
    weights = weights / np.sqrt(np.sum(weights * weights))
    return weights.reshape(TAPS, UPCH)


def filter_table():
    window = window_taps()
    span = GROUP + 16
    angle = 2.0 * np.pi * (np.arange(UPCH)[:, None] * np.arange(UPCH)[None, :] % UPCH) / UPCH
    cosine, sine = np.cos(angle), np.sin(angle)
    table = np.zeros((2, GROUP, UPCH, span, UPCH, 2))
    for frame in range(GROUP):
        for tap in range(TAPS):
            at = frame + 1 + tap
            table[0, frame, :, at, :, 0] = window[tap] * cosine
            table[0, frame, :, at, :, 1] = window[tap] * sine
            table[1, frame, :, at, :, 0] = -window[tap] * sine
            table[1, frame, :, at, :, 1] = window[tap] * cosine
    table = table.reshape(2 * ROWS, span * UPCH * 2).astype(np.float32)
    return table.astype(ml_dtypes.bfloat16)


def beam_matrix():
    rows = np.arange(NS)
    phase = rows[:, None] * rows[None, :] % NS
    angle = np.float32(2.0 * np.pi) * phase.astype(np.float32) / np.float32(NS)
    scale = np.float32(1.0 / np.sqrt(NS))
    cosine = np.cos(angle) * scale
    sine = np.sin(angle) * scale
    upper = np.concatenate([cosine, -sine], axis=1)
    lower = np.concatenate([sine, cosine], axis=1)
    return np.concatenate([upper, lower], axis=0).astype(ml_dtypes.bfloat16)


def kernel(
    n_freq, n_tm, groups, n_sets, x_ref, gain_ref, owner_ref, keep_ref, filt_ref, beam_ref, out_ref,
    xbuf, part, powers, arrived, place, outgoing,
    load_sem, halo_send, halo_recv, pol_send, pol_recv, set_send, set_recv, own_sem,
):
    freq = lax.axis_index("freq")
    tm = lax.axis_index("tm")
    pol = lax.axis_index("pol")
    half = groups // 2
    most = 2 * n_sets // n_freq
    columns = most * SET_BEAMS
    span = n_freq * columns

    loads = []
    for chunk in range(groups):
        load = pltpu.make_async_copy(x_ref.at[chunk], xbuf.at[chunk + 2], load_sem.at[chunk])
        load.start()
        loads.append(load)

    barrier = pltpu.get_barrier_semaphore()
    pl.semaphore_signal(barrier, inc=1, device_id={"pol": 1 - pol}, device_id_type=pl.DeviceIdType.MESH)
    for step in range(1, n_freq):
        pl.semaphore_signal(
            barrier, inc=1, device_id={"freq": lax.rem(freq + step, n_freq)}, device_id_type=pl.DeviceIdType.MESH
        )
    for step in range(1, n_tm):
        pl.semaphore_signal(
            barrier, inc=1, device_id={"tm": lax.rem(tm + step, n_tm)}, device_id_type=pl.DeviceIdType.MESH
        )
    pl.semaphore_wait(barrier, n_freq + n_tm - 1)

    def halo(chunk):
        return pltpu.make_async_remote_copy(
            src_ref=x_ref.at[groups - 2 + chunk],
            dst_ref=xbuf.at[chunk],
            send_sem=halo_send.at[chunk],
            recv_sem=halo_recv.at[chunk],
            device_id={"tm": lax.rem(tm + 1, n_tm)},
            device_id_type=pl.DeviceIdType.MESH,
        )

    @pl.when(tm < n_tm - 1)
    def _():
        halo(1).start()
        halo(0).start()

    @pl.when(tm == 0)
    def _():
        xbuf[0] = jnp.zeros(xbuf.shape[1:], xbuf.dtype)
        xbuf[1] = jnp.zeros(xbuf.shape[1:], xbuf.dtype)

    owner_row = owner_ref[...].astype(jnp.float32)
    s_row = lax.broadcasted_iota(jnp.int32, (n_sets, n_sets), 0)
    s_col = lax.broadcasted_iota(jnp.int32, (n_sets, n_sets), 1)
    spread = jnp.broadcast_to(owner_row, (n_sets, n_sets))
    owner_col = jnp.sum(jnp.where(s_row == s_col, spread, 0.0), axis=1, keepdims=True)
    same = jnp.logical_and(spread == owner_col, s_col < s_row)
    rank = jnp.sum(jnp.where(same, 1.0, 0.0), axis=1, keepdims=True)
    slot = (owner_col * most + rank).astype(jnp.int32)
    column = lax.broadcasted_iota(jnp.int32, (n_sets, span), 1)
    set_at = lax.broadcasted_iota(jnp.int32, (n_sets, span), 0)
    match = slot == column // SET_BEAMS
    beam_at = jnp.where(match, (set_at * SET_BEAMS + column % SET_BEAMS + 1).astype(jnp.float32), 0.0)
    beam_of = jnp.sum(beam_at, axis=0, keepdims=True).astype(jnp.int32) - 1
    keep = keep_ref[...].astype(jnp.float32)

    @pl.loop(0, BEAMS // 16)
    def _(step):
        first = pl.multiple_of(step * 16, 16)
        beam = lax.broadcasted_iota(jnp.int32, (16, span), 0) + first
        place[pl.ds(first, 16), :] = jnp.where(beam == beam_of, 1.0, 0.0).astype(jnp.bfloat16)

    def to_partner(g):
        return pltpu.make_async_remote_copy(
            src_ref=powers.at[g],
            dst_ref=arrived.at[g % half],
            send_sem=pol_send.at[g % half],
            recv_sem=pol_recv.at[g % half],
            device_id={"pol": 1 - pol},
            device_id_type=pl.DeviceIdType.MESH,
        )

    def to_owner(g, owner):
        rows = pl.ds(pl.multiple_of((g % half) * GROUP, GROUP), GROUP)
        return pltpu.make_async_remote_copy(
            src_ref=outgoing.at[g % half, owner],
            dst_ref=out_ref.at[rows, freq],
            send_sem=set_send.at[g % half, owner],
            recv_sem=set_recv.at[g % half, freq],
            device_id={"freq": owner},
            device_id_type=pl.DeviceIdType.MESH,
        )

    def from_source(slot_at, source):
        rows = pl.ds(slot_at * GROUP, GROUP)
        return pltpu.make_async_remote_copy(
            src_ref=outgoing.at[slot_at, source],
            dst_ref=out_ref.at[rows, source],
            send_sem=set_send.at[slot_at, source],
            recv_sem=set_recv.at[slot_at, source],
            device_id={"freq": source},
            device_id_type=pl.DeviceIdType.MESH,
        )

    def own_copy(g):
        rows = pl.ds(pl.multiple_of((g % half) * GROUP, GROUP), GROUP)
        return pltpu.make_async_copy(outgoing.at[g % half, freq], out_ref.at[rows, freq], own_sem.at[g % half])

    for load in loads:
        load.wait()

    @pl.loop(0, groups)
    def _(index):
        g = groups - 1 - index

        @pl.when(jnp.logical_and(g < 2, tm > 0))
        def _():
            halo(g).wait_recv()

        for y in range(CYL):
            total = jnp.dot(filt_ref[:, 0:WIDE], xbuf[g, y], preferred_element_type=jnp.float32)
            total += jnp.dot(filt_ref[:, WIDE : 2 * WIDE], xbuf[g + 1, y], preferred_element_type=jnp.float32)
            total += jnp.dot(filt_ref[:, 2 * WIDE : 3 * WIDE], xbuf[g + 2, y], preferred_element_type=jnp.float32)
            real, imag = total[:ROWS], total[ROWS:]
            gain_real = gain_ref[2 * y : 2 * y + 1, :]
            gain_imag = gain_ref[2 * y + 1 : 2 * y + 2, :]
            cal_real = (real * gain_real - imag * gain_imag).astype(jnp.bfloat16)
            cal_imag = (real * gain_imag + imag * gain_real).astype(jnp.bfloat16)
            calibrated = jnp.concatenate([cal_real, cal_imag], axis=1)
            part[y] = jnp.dot(calibrated, beam_ref[...], preferred_element_type=jnp.float32)

        @pl.loop(0, ROWS // 16)
        def _(step):
            rows = pl.ds(pl.multiple_of(step * 16, 16), 16)
            re = [part[y, rows, 0:NS] for y in range(CYL)]
            im = [part[y, rows, NS : 2 * NS] for y in range(CYL)]
            sum_re, sum_im = re[0] + re[2], im[0] + im[2]
            odd_re, odd_im = re[1] + re[3], im[1] + im[3]
            dif_re, dif_im = re[0] - re[2], im[0] - im[2]
            cross_re, cross_im = re[1] - re[3], im[1] - im[3]
            formed = (
                (sum_re + odd_re, sum_im + odd_im),
                (dif_re + cross_im, dif_im - cross_re),
                (sum_re - odd_re, sum_im - odd_im),
                (dif_re - cross_im, dif_im + cross_re),
            )
            for e, (f_re, f_im) in enumerate(formed):
                value = 0.25 * (f_re * f_re + f_im * f_im)
                powers[g, rows, e * NS : (e + 1) * NS] = value.astype(jnp.bfloat16)

        mine = g // half == pol

        @pl.when(jnp.logical_not(mine))
        def _():
            to_partner(g).start()

        @pl.when(mine)
        def _():
            to_partner(g).wait_recv()
            both = powers[g].astype(jnp.float32) + arrived[g % half].astype(jnp.float32)
            intensity = both.astype(jnp.bfloat16) * keep.astype(jnp.bfloat16)
            for owner in range(n_freq):
                block = jnp.dot(
                    intensity,
                    place[:, owner * columns : (owner + 1) * columns],
                    preferred_element_type=jnp.float32,
                )
                outgoing[g % half, owner] = block.astype(jnp.bfloat16).reshape(GROUP, UPCH, columns)
            for step in range(1, n_freq):
                to_owner(g, lax.rem(freq + step, n_freq)).start()
            own_copy(g).start()

    for slot_at in range(half):
        own_copy(slot_at).wait()
        to_partner(slot_at).wait_send()
        for step in range(1, n_freq):
            peer = lax.rem(freq + step, n_freq)
            from_source(slot_at, peer).wait_send()
            from_source(slot_at, peer).wait_recv()

    @pl.when(tm < n_tm - 1)
    def _():
        halo(0).wait_send()
        halo(1).wait_send()


def per_device(n_freq, n_tm, voltages, feed_gains, owner_table, keep_flags):
    samples = voltages.shape[2]
    groups = samples // (UPCH * GROUP)
    n_sets = owner_table.shape[0]
    columns = 2 * n_sets // n_freq * SET_BEAMS
    span = n_freq * columns
    half = groups // 2
    x = voltages.reshape(groups, GROUP * UPCH, CYL, 2, NS)
    x = x.transpose(0, 2, 1, 3, 4).reshape(groups, CYL, WIDE, NS)
    gains = feed_gains.reshape(CYL * 2, NS)
    vmem = pl.BlockSpec(memory_space=pltpu.VMEM)
    hbm = pl.BlockSpec(memory_space=pl.ANY)
    dma = pltpu.SemaphoreType.DMA
    out = pl.pallas_call(
        functools.partial(kernel, n_freq, n_tm, groups, n_sets),
        out_shape=jax.ShapeDtypeStruct((half * GROUP, n_freq, UPCH, columns), jnp.bfloat16),
        in_specs=[hbm, vmem, vmem, vmem, vmem, vmem],
        out_specs=hbm,
        scratch_shapes=[
            pltpu.VMEM((groups + 2, CYL, WIDE, NS), jnp.bfloat16),
            pltpu.VMEM((CYL, ROWS, 2 * NS), jnp.float32),
            pltpu.VMEM((groups, ROWS, BEAMS), jnp.bfloat16),
            pltpu.VMEM((half, ROWS, BEAMS), jnp.bfloat16),
            pltpu.VMEM((BEAMS, span), jnp.bfloat16),
            pltpu.VMEM((half, n_freq, GROUP, UPCH, columns), jnp.bfloat16),
            dma((groups,)),
            dma((2,)),
            dma((2,)),
            dma((half,)),
            dma((half,)),
            dma((half, n_freq)),
            dma((half, n_freq)),
            dma((half,)),
        ],
        compiler_params=pltpu.CompilerParams(
            collective_id=0, has_side_effects=True, vmem_limit_bytes=48 * 1024 * 1024
        ),
    )(
        x,
        gains,
        owner_table.reshape(1, n_sets),
        keep_flags.reshape(1, BEAMS),
        jnp.asarray(filter_table()),
        jnp.asarray(beam_matrix()),
    )
    return out.reshape(half * GROUP, n_freq * UPCH, columns)


def solution(mesh):
    return jax.shard_map(
        functools.partial(per_device, mesh.shape["freq"], mesh.shape["tm"]),
        mesh=mesh,
        in_specs=(
            P("pol", ("grp", "freq"), "tm", None, None, None),
            P(("grp", "freq"), "pol", None, None, None),
            P(),
            P(),
        ),
        out_specs=P(("grp", "tm", "pol"), None, "freq"),
        check_vma=False,
    )
```

```python
import functools

import jax
import jax.numpy as jnp
import ml_dtypes
import numpy as np
from jax import lax
from jax.experimental import pallas as pl
from jax.experimental.pallas import tpu as pltpu
from jax.sharding import PartitionSpec as P

NS = 256
CYL = 4
UPCH = 16
TAPS = 16
SET_BEAMS = 16
GROUP = 8
ROWS = GROUP * UPCH
WIDE = GROUP * UPCH * 2
BEAMS = CYL * NS


def window_taps():
    span = TAPS * UPCH
    steps = np.arange(span, dtype=np.float64)
    weights = np.sinc((steps - (span - 1) / 2.0) / UPCH) * np.sin(np.pi * (steps + 0.5) / span) ** 2
    weights = weights / np.sqrt(np.sum(weights * weights))
    return weights.reshape(TAPS, UPCH)


def filter_table():
    window = window_taps()
    span = GROUP + 16
    angle = 2.0 * np.pi * (np.arange(UPCH)[:, None] * np.arange(UPCH)[None, :] % UPCH) / UPCH
    cosine, sine = np.cos(angle), np.sin(angle)
    table = np.zeros((2, GROUP, UPCH, span, UPCH, 2))
    for frame in range(GROUP):
        for tap in range(TAPS):
            at = frame + 1 + tap
            table[0, frame, :, at, :, 0] = window[tap] * cosine
            table[0, frame, :, at, :, 1] = window[tap] * sine
            table[1, frame, :, at, :, 0] = -window[tap] * sine
            table[1, frame, :, at, :, 1] = window[tap] * cosine
    table = table.reshape(2 * ROWS, span * UPCH * 2).astype(np.float32)
    return table.astype(ml_dtypes.bfloat16)


def beam_matrix():
    rows = np.arange(NS)
    phase = rows[:, None] * rows[None, :] % NS
    angle = np.float32(2.0 * np.pi) * phase.astype(np.float32) / np.float32(NS)
    scale = np.float32(1.0 / np.sqrt(NS))
    cosine = np.cos(angle) * scale
    sine = np.sin(angle) * scale
    upper = np.concatenate([cosine, -sine], axis=1)
    lower = np.concatenate([sine, cosine], axis=1)
    return np.concatenate([upper, lower], axis=0).astype(ml_dtypes.bfloat16)


def kernel(
    n_freq, n_tm, groups, n_sets, x_ref, gain_ref, owner_ref, keep_ref, filt_ref, beam_ref, out_ref,
    raw, xbuf, part, powers, arrived, place, outgoing,
    load_sem, halo_send, halo_recv, pol_send, pol_recv, set_send, set_recv, own_sem,
):
    freq = lax.axis_index("freq")
    tm = lax.axis_index("tm")
    pol = lax.axis_index("pol")
    half = groups // 2
    most = 2 * n_sets // n_freq
    columns = most * SET_BEAMS
    span = n_freq * columns

    loads = []
    for chunk in range(groups):
        load = pltpu.make_async_copy(x_ref.at[chunk], raw.at[chunk + 2], load_sem.at[chunk])
        load.start()
        loads.append(load)

    barrier = pltpu.get_barrier_semaphore()
    pl.semaphore_signal(barrier, inc=1, device_id={"pol": 1 - pol}, device_id_type=pl.DeviceIdType.MESH)
    for step in range(1, n_freq):
        pl.semaphore_signal(
            barrier, inc=1, device_id={"freq": lax.rem(freq + step, n_freq)}, device_id_type=pl.DeviceIdType.MESH
        )
    for step in range(1, n_tm):
        pl.semaphore_signal(
            barrier, inc=1, device_id={"tm": lax.rem(tm + step, n_tm)}, device_id_type=pl.DeviceIdType.MESH
        )
    pl.semaphore_wait(barrier, n_freq + n_tm - 1)

    def halo(chunk):
        first = UPCH * (1 - chunk)
        rows = pl.ds(first, ROWS - first)
        return pltpu.make_async_remote_copy(
            src_ref=x_ref.at[groups - 2 + chunk, rows],
            dst_ref=raw.at[chunk, rows],
            send_sem=halo_send.at[chunk],
            recv_sem=halo_recv.at[chunk],
            device_id={"tm": lax.rem(tm + 1, n_tm)},
            device_id_type=pl.DeviceIdType.MESH,
        )

    def reorder(chunk):
        for y in range(CYL):
            xbuf[chunk, y] = raw[chunk, :, y].reshape(WIDE, NS)

    @pl.when(tm < n_tm - 1)
    def _():
        halo(1).start()
        halo(0).start()

    raw[0, 0:UPCH] = jnp.zeros((UPCH, CYL, 2, NS), raw.dtype)

    @pl.when(tm == 0)
    def _():
        raw[0, UPCH:] = jnp.zeros((ROWS - UPCH, CYL, 2, NS), raw.dtype)
        raw[1] = jnp.zeros((ROWS, CYL, 2, NS), raw.dtype)

    owner_row = owner_ref[...].astype(jnp.float32)
    s_row = lax.broadcasted_iota(jnp.int32, (n_sets, n_sets), 0)
    s_col = lax.broadcasted_iota(jnp.int32, (n_sets, n_sets), 1)
    spread = jnp.broadcast_to(owner_row, (n_sets, n_sets))
    owner_col = jnp.sum(jnp.where(s_row == s_col, spread, 0.0), axis=1, keepdims=True)
    same = jnp.logical_and(spread == owner_col, s_col < s_row)
    rank = jnp.sum(jnp.where(same, 1.0, 0.0), axis=1, keepdims=True)
    slot = (owner_col * most + rank).astype(jnp.int32)
    column = lax.broadcasted_iota(jnp.int32, (n_sets, span), 1)
    set_at = lax.broadcasted_iota(jnp.int32, (n_sets, span), 0)
    match = slot == column // SET_BEAMS
    beam_at = jnp.where(match, (set_at * SET_BEAMS + column % SET_BEAMS + 1).astype(jnp.float32), 0.0)
    beam_of = jnp.sum(beam_at, axis=0, keepdims=True).astype(jnp.int32) - 1
    keep = keep_ref[...].astype(jnp.float32)

    @pl.loop(0, BEAMS // 16)
    def _(step):
        first = pl.multiple_of(step * 16, 16)
        beam = lax.broadcasted_iota(jnp.int32, (16, span), 0) + first
        place[pl.ds(first, 16), :] = jnp.where(beam == beam_of, 1.0, 0.0).astype(jnp.bfloat16)

    def to_partner(g):
        return pltpu.make_async_remote_copy(
            src_ref=powers.at[g],
            dst_ref=arrived.at[g % half],
            send_sem=pol_send.at[g % half],
            recv_sem=pol_recv.at[g % half],
            device_id={"pol": 1 - pol},
            device_id_type=pl.DeviceIdType.MESH,
        )

    def to_owner(g, owner):
        rows = pl.ds(pl.multiple_of((g % half) * GROUP, GROUP), GROUP)
        return pltpu.make_async_remote_copy(
            src_ref=outgoing.at[g % half, owner],
            dst_ref=out_ref.at[rows, freq],
            send_sem=set_send.at[g % half, owner],
            recv_sem=set_recv.at[g % half, freq],
            device_id={"freq": owner},
            device_id_type=pl.DeviceIdType.MESH,
        )

    def from_source(slot_at, source):
        rows = pl.ds(slot_at * GROUP, GROUP)
        return pltpu.make_async_remote_copy(
            src_ref=outgoing.at[slot_at, source],
            dst_ref=out_ref.at[rows, source],
            send_sem=set_send.at[slot_at, source],
            recv_sem=set_recv.at[slot_at, source],
            device_id={"freq": source},
            device_id_type=pl.DeviceIdType.MESH,
        )

    def own_copy(g):
        rows = pl.ds(pl.multiple_of((g % half) * GROUP, GROUP), GROUP)
        return pltpu.make_async_copy(outgoing.at[g % half, freq], out_ref.at[rows, freq], own_sem.at[g % half])

    for load in loads:
        load.wait()
    reorder(groups)
    reorder(groups + 1)

    @pl.loop(0, groups)
    def _(index):
        g = groups - 1 - index

        @pl.when(jnp.logical_and(g == 1, tm > 0))
        def _():
            halo(1).wait_recv()

        @pl.when(jnp.logical_and(g == 0, tm > 0))
        def _():
            halo(0).wait_recv()

        reorder(g)

        for y in range(CYL):
            total = jnp.dot(filt_ref[:, 0:WIDE], xbuf[g, y], preferred_element_type=jnp.float32)
            total += jnp.dot(filt_ref[:, WIDE : 2 * WIDE], xbuf[g + 1, y], preferred_element_type=jnp.float32)
            total += jnp.dot(filt_ref[:, 2 * WIDE : 3 * WIDE], xbuf[g + 2, y], preferred_element_type=jnp.float32)
            real, imag = total[:ROWS], total[ROWS:]
            gain_real = gain_ref[2 * y : 2 * y + 1, :]
            gain_imag = gain_ref[2 * y + 1 : 2 * y + 2, :]
            cal_real = (real * gain_real - imag * gain_imag).astype(jnp.bfloat16)
            cal_imag = (real * gain_imag + imag * gain_real).astype(jnp.bfloat16)
            calibrated = jnp.concatenate([cal_real, cal_imag], axis=1)
            part[y] = jnp.dot(calibrated, beam_ref[...], preferred_element_type=jnp.float32)

        @pl.loop(0, ROWS // 16)
        def _(step):
            rows = pl.ds(pl.multiple_of(step * 16, 16), 16)
            re = [part[y, rows, 0:NS] for y in range(CYL)]
            im = [part[y, rows, NS : 2 * NS] for y in range(CYL)]
            sum_re, sum_im = re[0] + re[2], im[0] + im[2]
            odd_re, odd_im = re[1] + re[3], im[1] + im[3]
            dif_re, dif_im = re[0] - re[2], im[0] - im[2]
            cross_re, cross_im = re[1] - re[3], im[1] - im[3]
            formed = (
                (sum_re + odd_re, sum_im + odd_im),
                (dif_re + cross_im, dif_im - cross_re),
                (sum_re - odd_re, sum_im - odd_im),
                (dif_re - cross_im, dif_im + cross_re),
            )
            for e, (f_re, f_im) in enumerate(formed):
                value = 0.25 * (f_re * f_re + f_im * f_im)
                powers[g, rows, e * NS : (e + 1) * NS] = value.astype(jnp.bfloat16)

        mine = g // half == pol

        @pl.when(jnp.logical_not(mine))
        def _():
            to_partner(g).start()

        @pl.when(mine)
        def _():
            to_partner(g).wait_recv()
            both = powers[g].astype(jnp.float32) + arrived[g % half].astype(jnp.float32)
            intensity = both.astype(jnp.bfloat16) * keep.astype(jnp.bfloat16)
            for owner in range(n_freq):
                block = jnp.dot(
                    intensity,
                    place[:, owner * columns : (owner + 1) * columns],
                    preferred_element_type=jnp.float32,
                )
                outgoing[g % half, owner] = block.astype(jnp.bfloat16).reshape(GROUP, UPCH, columns)
            for step in range(1, n_freq):
                to_owner(g, lax.rem(freq + step, n_freq)).start()
            own_copy(g).start()

    for slot_at in range(half):
        own_copy(slot_at).wait()
        to_partner(slot_at).wait_send()
        for step in range(1, n_freq):
            peer = lax.rem(freq + step, n_freq)
            from_source(slot_at, peer).wait_send()
            from_source(slot_at, peer).wait_recv()

    @pl.when(tm < n_tm - 1)
    def _():
        halo(0).wait_send()
        halo(1).wait_send()


def per_device(n_freq, n_tm, voltages, feed_gains, owner_table, keep_flags):
    samples = voltages.shape[2]
    groups = samples // (UPCH * GROUP)
    n_sets = owner_table.shape[0]
    columns = 2 * n_sets // n_freq * SET_BEAMS
    span = n_freq * columns
    half = groups // 2
    x = voltages.reshape(groups, ROWS, CYL, 2, NS)
    gains = feed_gains.reshape(CYL * 2, NS)
    vmem = pl.BlockSpec(memory_space=pltpu.VMEM)
    hbm = pl.BlockSpec(memory_space=pl.ANY)
    dma = pltpu.SemaphoreType.DMA
    out = pl.pallas_call(
        functools.partial(kernel, n_freq, n_tm, groups, n_sets),
        out_shape=jax.ShapeDtypeStruct((half * GROUP, n_freq, UPCH, columns), jnp.bfloat16),
        in_specs=[hbm, vmem, vmem, vmem, vmem, vmem],
        out_specs=hbm,
        scratch_shapes=[
            pltpu.VMEM((groups + 2, ROWS, CYL, 2, NS), jnp.bfloat16),
            pltpu.VMEM((groups + 2, CYL, WIDE, NS), jnp.bfloat16),
            pltpu.VMEM((CYL, ROWS, 2 * NS), jnp.float32),
            pltpu.VMEM((groups, ROWS, BEAMS), jnp.bfloat16),
            pltpu.VMEM((half, ROWS, BEAMS), jnp.bfloat16),
            pltpu.VMEM((BEAMS, span), jnp.bfloat16),
            pltpu.VMEM((half, n_freq, GROUP, UPCH, columns), jnp.bfloat16),
            dma((groups,)),
            dma((2,)),
            dma((2,)),
            dma((half,)),
            dma((half,)),
            dma((half, n_freq)),
            dma((half, n_freq)),
            dma((half,)),
        ],
        compiler_params=pltpu.CompilerParams(
            collective_id=0, has_side_effects=True, vmem_limit_bytes=48 * 1024 * 1024
        ),
    )(
        x,
        gains,
        owner_table.reshape(1, n_sets),
        keep_flags.reshape(1, BEAMS),
        jnp.asarray(filter_table()),
        jnp.asarray(beam_matrix()),
    )
    return out.reshape(half * GROUP, n_freq * UPCH, columns)


def solution(mesh):
    return jax.shard_map(
        functools.partial(per_device, mesh.shape["freq"], mesh.shape["tm"]),
        mesh=mesh,
        in_specs=(
            P("pol", ("grp", "freq"), "tm", None, None, None),
            P(("grp", "freq"), "pol", None, None, None),
            P(),
            P(),
        ),
        out_specs=P(("grp", "tm", "pol"), None, "freq"),
        check_vma=False,
    )
```

```python
import functools

import jax
import jax.numpy as jnp
import ml_dtypes
import numpy as np
from jax import lax
from jax.experimental import pallas as pl
from jax.experimental.pallas import tpu as pltpu
from jax.sharding import PartitionSpec as P

NS = 256
CYL = 4
UPCH = 16
TAPS = 16
SET_BEAMS = 16
GROUP = 8
ROWS = GROUP * UPCH
WIDE = GROUP * UPCH * 2
BEAMS = CYL * NS


def window_taps():
    span = TAPS * UPCH
    steps = np.arange(span, dtype=np.float64)
    weights = np.sinc((steps - (span - 1) / 2.0) / UPCH) * np.sin(np.pi * (steps + 0.5) / span) ** 2
    weights = weights / np.sqrt(np.sum(weights * weights))
    return weights.reshape(TAPS, UPCH)


def filter_table():
    window = window_taps()
    span = GROUP + 16
    angle = 2.0 * np.pi * (np.arange(UPCH)[:, None] * np.arange(UPCH)[None, :] % UPCH) / UPCH
    cosine, sine = np.cos(angle), np.sin(angle)
    table = np.zeros((2, GROUP, UPCH, span, UPCH, 2))
    for frame in range(GROUP):
        for tap in range(TAPS):
            at = frame + 1 + tap
            table[0, frame, :, at, :, 0] = window[tap] * cosine
            table[0, frame, :, at, :, 1] = window[tap] * sine
            table[1, frame, :, at, :, 0] = -window[tap] * sine
            table[1, frame, :, at, :, 1] = window[tap] * cosine
    table = table.reshape(2 * ROWS, span * UPCH * 2).astype(np.float32)
    return table.astype(ml_dtypes.bfloat16)


def beam_matrix():
    rows = np.arange(NS)
    phase = rows[:, None] * rows[None, :] % NS
    angle = np.float32(2.0 * np.pi) * phase.astype(np.float32) / np.float32(NS)
    scale = np.float32(1.0 / np.sqrt(NS))
    cosine = np.cos(angle) * scale
    sine = np.sin(angle) * scale
    upper = np.concatenate([cosine, -sine], axis=1)
    lower = np.concatenate([sine, cosine], axis=1)
    return np.concatenate([upper, lower], axis=0).astype(ml_dtypes.bfloat16)


def kernel(
    n_freq, n_tm, groups, n_sets, x_ref, gain_hbm, owner_hbm, keep_hbm, filt_hbm, beam_hbm, out_ref,
    gain_ref, owner_ref, keep_ref, filt_ref, beam_ref,
    raw, xbuf, part, powers, arrived, place, outgoing, handed, given,
    load_sem, table_sem, halo_send, halo_recv, pol_send, pol_recv, hand_send, hand_recv, set_send, set_recv, own_sem,
):
    freq = lax.axis_index("freq")
    tm = lax.axis_index("tm")
    pol = lax.axis_index("pol")
    has_next = tm < n_tm - 1
    has_prev = tm > 0
    half = groups // 2
    most = 2 * n_sets // n_freq
    columns = most * SET_BEAMS
    span = n_freq * columns
    mesh_id = pl.DeviceIdType.MESH

    barrier = pltpu.get_barrier_semaphore()
    pl.semaphore_signal(barrier, inc=1, device_id={"pol": 1 - pol}, device_id_type=mesh_id)
    for step in range(1, n_freq):
        pl.semaphore_signal(barrier, inc=1, device_id={"freq": lax.rem(freq + step, n_freq)}, device_id_type=mesh_id)
    for step in range(1, n_tm):
        pl.semaphore_signal(barrier, inc=1, device_id={"tm": lax.rem(tm + step, n_tm)}, device_id_type=mesh_id)

    pairs = ((owner_hbm, owner_ref), (keep_hbm, keep_ref), (filt_hbm, filt_ref), (gain_hbm, gain_ref), (beam_hbm, beam_ref))
    tables = [pltpu.make_async_copy(src, dst, table_sem.at[i]) for i, (src, dst) in enumerate(pairs)]
    loads = [pltpu.make_async_copy(x_ref.at[i], raw.at[i + 2], load_sem.at[i]) for i in range(groups)]
    tables[0].start()
    tables[1].start()
    for load in loads[::-1]:
        load.start()
    for table in tables[2:]:
        table.start()

    pl.semaphore_wait(barrier, n_freq + n_tm - 1)

    def forward():
        rows = pl.ds(UPCH, ROWS - UPCH)
        return pltpu.make_async_remote_copy(
            src_ref=x_ref.at[groups - 1, rows],
            dst_ref=raw.at[1, rows],
            send_sem=halo_send.at[0],
            recv_sem=halo_recv.at[0],
            device_id={"tm": lax.rem(tm + 1, n_tm)},
            device_id_type=mesh_id,
        )

    def backward():
        return pltpu.make_async_remote_copy(
            src_ref=x_ref.at[0],
            dst_ref=raw.at[groups + 2],
            send_sem=halo_send.at[1],
            recv_sem=halo_recv.at[1],
            device_id={"tm": lax.rem(tm + n_tm - 1, n_tm)},
            device_id_type=mesh_id,
        )

    def hand_over():
        return pltpu.make_async_remote_copy(
            src_ref=handed,
            dst_ref=given,
            send_sem=hand_send,
            recv_sem=hand_recv,
            device_id={"tm": lax.rem(tm + 1, n_tm)},
            device_id_type=mesh_id,
        )

    def reorder(chunk):
        for y in range(CYL):
            xbuf[chunk, y] = raw[chunk, :, y].reshape(WIDE, NS)

    @pl.when(has_next)
    def _():
        forward().start()

    @pl.when(has_prev)
    def _():
        backward().start()

    raw[1, 0:UPCH] = jnp.zeros((UPCH, CYL, 2, NS), raw.dtype)

    @pl.when(tm == 0)
    def _():
        raw[0] = jnp.zeros((ROWS, CYL, 2, NS), raw.dtype)
        raw[1, UPCH:] = jnp.zeros((ROWS - UPCH, CYL, 2, NS), raw.dtype)

    tables[0].wait()
    tables[1].wait()
    owner_row = owner_ref[...].astype(jnp.float32)
    s_row = lax.broadcasted_iota(jnp.int32, (n_sets, n_sets), 0)
    s_col = lax.broadcasted_iota(jnp.int32, (n_sets, n_sets), 1)
    spread = jnp.broadcast_to(owner_row, (n_sets, n_sets))
    owner_col = jnp.sum(jnp.where(s_row == s_col, spread, 0.0), axis=1, keepdims=True)
    same = jnp.logical_and(spread == owner_col, s_col < s_row)
    rank = jnp.sum(jnp.where(same, 1.0, 0.0), axis=1, keepdims=True)
    slot = (owner_col * most + rank).astype(jnp.int32)
    column = lax.broadcasted_iota(jnp.int32, (n_sets, span), 1)
    set_at = lax.broadcasted_iota(jnp.int32, (n_sets, span), 0)
    match = slot == column // SET_BEAMS
    beam_at = jnp.where(match, (set_at * SET_BEAMS + column % SET_BEAMS + 1).astype(jnp.float32), 0.0)
    beam_of = jnp.sum(beam_at, axis=0, keepdims=True).astype(jnp.int32) - 1

    @pl.loop(0, BEAMS // 16)
    def _(step):
        first = pl.multiple_of(step * 16, 16)
        beam = lax.broadcasted_iota(jnp.int32, (16, span), 0) + first
        place[pl.ds(first, 16), :] = jnp.where(beam == beam_of, 1.0, 0.0).astype(jnp.bfloat16)

    def to_partner(g, at):
        return pltpu.make_async_remote_copy(
            src_ref=powers.at[g],
            dst_ref=arrived.at[at],
            send_sem=pol_send.at[at],
            recv_sem=pol_recv.at[at],
            device_id={"pol": 1 - pol},
            device_id_type=mesh_id,
        )

    def to_owner(at, owner):
        rows = pl.ds(at * GROUP, GROUP)
        return pltpu.make_async_remote_copy(
            src_ref=outgoing.at[at, owner],
            dst_ref=out_ref.at[rows, freq],
            send_sem=set_send.at[at, owner],
            recv_sem=set_recv.at[at, freq],
            device_id={"freq": owner},
            device_id_type=mesh_id,
        )

    def from_source(at, source):
        rows = pl.ds(at * GROUP, GROUP)
        return pltpu.make_async_remote_copy(
            src_ref=outgoing.at[at, source],
            dst_ref=out_ref.at[rows, source],
            send_sem=set_send.at[at, source],
            recv_sem=set_recv.at[at, source],
            device_id={"freq": source},
            device_id_type=mesh_id,
        )

    def own_copy(at):
        rows = pl.ds(at * GROUP, GROUP)
        return pltpu.make_async_copy(outgoing.at[at, freq], out_ref.at[rows, freq], own_sem.at[at])

    def form_powers(g):
        for y in range(CYL):
            total = jnp.dot(filt_ref[:, 0:WIDE], xbuf[g, y], preferred_element_type=jnp.float32)
            total += jnp.dot(filt_ref[:, WIDE : 2 * WIDE], xbuf[g + 1, y], preferred_element_type=jnp.float32)
            total += jnp.dot(filt_ref[:, 2 * WIDE : 3 * WIDE], xbuf[g + 2, y], preferred_element_type=jnp.float32)
            real, imag = total[:ROWS], total[ROWS:]
            gain_real = gain_ref[y, 0:1, :]
            gain_imag = gain_ref[y, 1:2, :]
            cal_real = (real * gain_real - imag * gain_imag).astype(jnp.bfloat16)
            cal_imag = (real * gain_imag + imag * gain_real).astype(jnp.bfloat16)
            calibrated = jnp.concatenate([cal_real, cal_imag], axis=1)
            part[y] = jnp.dot(calibrated, beam_ref[...], preferred_element_type=jnp.float32)

        @pl.loop(0, ROWS // 16)
        def _(step):
            rows = pl.ds(pl.multiple_of(step * 16, 16), 16)
            re = [part[y, rows, 0:NS] for y in range(CYL)]
            im = [part[y, rows, NS : 2 * NS] for y in range(CYL)]
            sum_re, sum_im = re[0] + re[2], im[0] + im[2]
            odd_re, odd_im = re[1] + re[3], im[1] + im[3]
            dif_re, dif_im = re[0] - re[2], im[0] - im[2]
            cross_re, cross_im = re[1] - re[3], im[1] - im[3]
            formed = (
                (sum_re + odd_re, sum_im + odd_im),
                (dif_re + cross_im, dif_im - cross_re),
                (sum_re - odd_re, sum_im - odd_im),
                (dif_re - cross_im, dif_im + cross_re),
            )
            for e, (f_re, f_im) in enumerate(formed):
                value = 0.25 * (f_re * f_re + f_im * f_im)
                powers[g, rows, e * NS : (e + 1) * NS] = value.astype(jnp.bfloat16)

    def both_pols(g, at):
        to_partner(g, at).wait_recv()
        both = powers[g].astype(jnp.float32) + arrived[at].astype(jnp.float32)
        return both.astype(jnp.bfloat16) * keep_ref[...].astype(jnp.bfloat16)

    def regroup(intensity, at):
        for step in range(n_freq):
            owner = lax.rem(freq + step, n_freq) if step else freq
            first = pl.multiple_of(owner * columns, columns)
            block = jnp.dot(intensity, place[:, pl.ds(first, columns)], preferred_element_type=jnp.float32)
            outgoing[at, owner] = block.astype(jnp.bfloat16).reshape(GROUP, UPCH, columns)
            if step:
                to_owner(at, owner).start()
            else:
                own_copy(at).start()

    for load in loads:
        load.wait()
    for table in tables[2:]:
        table.wait()
    reorder(groups)
    reorder(groups + 1)

    @pl.loop(0, groups - 1)
    def _(index):
        g = groups - 1 - index

        @pl.when(jnp.logical_and(g == 1, has_prev))
        def _():
            forward().wait_recv()

        reorder(g)
        form_powers(g)
        mine = g // half == pol

        @pl.when(jnp.logical_not(mine))
        def _():
            to_partner(g, g % half).start()

        @pl.when(mine)
        def _():
            regroup(both_pols(g, g % half), g % half)

    @pl.loop(0, 2)
    def _(index):
        g = groups * (1 - index)
        at = half * (1 - index)

        @pl.when(jnp.logical_or(jnp.logical_and(index == 0, has_next), jnp.logical_and(index == 1, tm == 0)))
        def _():
            @pl.when(index == 0)
            def _():
                backward().wait_recv()
                reorder(groups + 2)

            @pl.when(index == 1)
            def _():
                reorder(0)
                reorder(1)

            form_powers(g)

            @pl.when(pol == 1)
            def _():
                to_partner(g, at).start()

            @pl.when(pol == 0)
            def _():
                @pl.when(index == 0)
                def _():
                    handed[...] = both_pols(g, at)
                    hand_over().start()

                @pl.when(index == 1)
                def _():
                    given[...] = both_pols(g, at)

        @pl.when(jnp.logical_and(index == 1, pol == 0))
        def _():
            @pl.when(has_prev)
            def _():
                hand_over().wait_recv()

            regroup(given[...], 0)

    for at in range(half):
        own_copy(at).wait()
        for step in range(1, n_freq):
            peer = lax.rem(freq + step, n_freq)
            from_source(at, peer).wait_send()
            from_source(at, peer).wait_recv()
        if at:
            to_partner(at, at).wait_send()

    @pl.when(jnp.logical_or(pol == 0, tm == 0))
    def _():
        to_partner(0, 0).wait_send()

    @pl.when(has_next)
    def _():
        forward().wait_send()

        @pl.when(pol == 1)
        def _():
            to_partner(groups, half).wait_send()

        @pl.when(pol == 0)
        def _():
            hand_over().wait_send()

    @pl.when(has_prev)
    def _():
        backward().wait_send()


def per_device(n_freq, n_tm, voltages, feed_gains, owner_table, keep_flags):
    samples = voltages.shape[2]
    groups = samples // (UPCH * GROUP)
    n_sets = owner_table.shape[0]
    columns = 2 * n_sets // n_freq * SET_BEAMS
    span = n_freq * columns
    half = groups // 2
    x = voltages.reshape(groups, ROWS, CYL, 2, NS)
    gains = feed_gains.reshape(CYL, 2, NS)
    hbm = pl.BlockSpec(memory_space=pl.ANY)
    dma = pltpu.SemaphoreType.DMA
    out = pl.pallas_call(
        functools.partial(kernel, n_freq, n_tm, groups, n_sets),
        out_shape=jax.ShapeDtypeStruct((half * GROUP, n_freq, UPCH, columns), jnp.bfloat16),
        in_specs=[hbm] * 6,
        out_specs=hbm,
        scratch_shapes=[
            pltpu.VMEM((CYL, 2, NS), jnp.float32),
            pltpu.VMEM((1, n_sets), jnp.int32),
            pltpu.VMEM((1, BEAMS), jnp.int32),
            pltpu.VMEM((2 * ROWS, 3 * WIDE), jnp.bfloat16),
            pltpu.VMEM((2 * NS, 2 * NS), jnp.bfloat16),
            pltpu.VMEM((groups + 3, ROWS, CYL, 2, NS), jnp.bfloat16),
            pltpu.VMEM((groups + 3, CYL, WIDE, NS), jnp.bfloat16),
            pltpu.VMEM((CYL, ROWS, 2 * NS), jnp.float32),
            pltpu.VMEM((groups + 1, ROWS, BEAMS), jnp.bfloat16),
            pltpu.VMEM((half + 1, ROWS, BEAMS), jnp.bfloat16),
            pltpu.VMEM((BEAMS, span), jnp.bfloat16),
            pltpu.VMEM((half, n_freq, GROUP, UPCH, columns), jnp.bfloat16),
            pltpu.VMEM((ROWS, BEAMS), jnp.bfloat16),
            pltpu.VMEM((ROWS, BEAMS), jnp.bfloat16),
            dma((groups,)),
            dma((5,)),
            dma((2,)),
            dma((2,)),
            dma((half + 1,)),
            dma((half + 1,)),
            dma(()),
            dma(()),
            dma((half, n_freq)),
            dma((half, n_freq)),
            dma((half,)),
        ],
        compiler_params=pltpu.CompilerParams(
            collective_id=0, has_side_effects=True, vmem_limit_bytes=58 * 1024 * 1024
        ),
    )(
        x,
        gains,
        owner_table.reshape(1, n_sets),
        keep_flags.reshape(1, BEAMS),
        jnp.asarray(filter_table()),
        jnp.asarray(beam_matrix()),
    )
    return out.reshape(half * GROUP, n_freq * UPCH, columns)


def solution(mesh):
    return jax.shard_map(
        functools.partial(per_device, mesh.shape["freq"], mesh.shape["tm"]),
        mesh=mesh,
        in_specs=(
            P("pol", ("grp", "freq"), "tm", None, None, None),
            P(("grp", "freq"), "pol", None, None, None),
            P(),
            P(),
        ),
        out_specs=P(("grp", "tm", "pol"), None, "freq"),
        check_vma=False,
    )
```
